32 devices in a mesh: groups: 2 (over x), fsdp: 16 (over z, y, core).
Axes of the slice: x: 2, y: 2, z: 4, core: 2. Of those that a mesh axis runs over, the one named last changes fastest.
Arguments:
- tokens: bfloat16 [32, 128, 4096], P(('groups', 'fsdp')), parts along dimension 0, may hold values from -30 to 30
- cotangent: bfloat16 [32, 128, 4096], P(('groups', 'fsdp')), parts along dimension 0, may hold values from -6 to 6
- block_lang: int32 [32], P('groups'), parts along dimension 0, may hold values from 0 to 3, as said below
- gain: float32 [4096], P('fsdp'), may hold values from 0.1 to 1.9
- w_down: bfloat16 [4096, 4096], P(None, 'fsdp'), may hold values from -0.09375 to 0.09375
- w_up: bfloat16 [4096, 4096], P('fsdp'), may hold values from -0.1875 to 0.1875
Outputs:
- adapted: bfloat16 [32, 128, 4096], P(('groups', 'fsdp')), parts along dimension 0
- x_grad: bfloat16 [32, 128, 4096], P(('groups', 'fsdp')), parts along dimension 0
- grad_down: bfloat16 [8192, 4096], P('groups', 'fsdp'), parts along dimension 0
- grad_up: bfloat16 [8192, 4096], P(('groups', 'fsdp')), parts along dimension 0
- grad_gain: float32 [8192], P(('groups', 'fsdp')), parts along dimension 0
The draws below stay inside these ranges and needn't reach their ends.
There are 2 independent parts, one for each index of `groups`. The reference program is written for one: setup_inputs(seed, part) draws one part's arguments, and reference() takes and returns one part's arrays. A program takes and returns all parts, laid end to end along the dimension named above; an argument that names none is the same for every part. Nothing has to cross between parts.
Inputs may be any that keep to these rules, and one draw needn't show every extreme that they name: `block_lang`: exactly one language, drawn from the seed, labels 6 blocks; the other 3 languages share the remaining 16 - 6 blocks as evenly as possible, their counts differing by at most one.
All inputs are finite; a program needn't handle non-finite values.
Results may differ from the reference program's by a relative error of at most 0.0061.
Values may be sent and summed in bfloat16 or wider, within the bound.
A program may use at most 192 MiB of HBM per device.

```python
import math
import jax
import jax.numpy as jnp
from jax import lax

D = 4096
R = 1024
OWN = 4
BLOCK = 128
MOSTB = 6
LANGS = 4
BLOCKS = 16
TOKENS = 2048


def draw_tokens(key, part):
    key = jax.random.fold_in(key, 5)
    subkeys = jax.random.split(key, 3)
    base = jax.random.truncated_normal(subkeys[0], -4.0, 4.0, (BLOCKS, BLOCK, D), jnp.float32)
    row_scale = jnp.exp(jax.random.uniform(subkeys[1], (BLOCKS, BLOCK, 1), jnp.float32, math.log(0.3), math.log(3.0)))
    col_scale = jnp.exp(jax.random.uniform(subkeys[2], (D,), jnp.float32, math.log(0.6), math.log(1.7)))
    values = base * row_scale * col_scale
    return values.astype(jnp.bfloat16)


def draw_block_lang(key, part):
    key = jax.random.fold_in(key, 11)
    subkeys = jax.random.split(key, 3)
    hot_lang = jax.random.randint(subkeys[0], (), 0, LANGS)
    others = jax.random.permutation(subkeys[1], LANGS - 1).astype(jnp.int32)
    spread = others[jnp.arange(BLOCKS - MOSTB) % (LANGS - 1)]
    spread = spread + (spread >= hot_lang).astype(jnp.int32)
    labels = jnp.concatenate([jnp.full((MOSTB,), hot_lang, jnp.int32), spread.astype(jnp.int32)])
    return labels[jax.random.permutation(subkeys[2], BLOCKS)]


def raised(values, rng, source, target, blocks, factor):
    def block_of(position):
        return (jnp.arange(values.shape[position]) // (values.shape[position] // blocks)).reshape((-1,) + (1,) * (values.ndim - 1 - position))

    near = jax.random.permutation(rng, blocks)[block_of(target)]
    second = (block_of(target) + blocks // 2) % blocks
    return jnp.where((block_of(source) == near) | (block_of(source) == second), factor * values, values)


def shard_levels(own_key, extent, cuts, smallest, high):
    factor_of, own = 1.0, jax.random.fold_in(own_key, 6)
    for axis_at, shards_of in cuts:
        steps = jnp.exp(jax.random.uniform(jax.random.fold_in(own, axis_at), (shards_of,), jnp.float32, smallest / len(cuts), high / len(cuts)))
        factor_of = factor_of * jnp.repeat(steps, extent[axis_at] // shards_of).reshape([-1 if axis == axis_at else 1 for axis in range(len(extent))])
    return factor_of


def noise(stream_key, shape, scale, most, shards=(), dtype=jnp.bfloat16):
    result = scale * jax.random.normal(stream_key, shape, jnp.float32)
    if shards:
        result = result * shard_levels(stream_key, shape, shards, -0.22, 0.18)
    return jnp.clip(result, -most, most).astype(dtype)


def bell_draw_with(rng, extent, scale, reach, cuts, heavy, kind=jnp.bfloat16):
    result = scale * jax.random.normal(rng, extent, jnp.float32)
    if cuts:
        result = result * shard_levels(rng, extent, cuts, -0.22, 0.18)
    return jnp.clip(raised(result, jax.random.fold_in(rng, 3), *heavy), -reach, reach).astype(kind)


def setup_inputs(seed: int = 0, part: int = 0) -> dict:
    streams_of = jax.random.split(jax.random.key(seed), 7)
    part_keys = jax.random.split(jax.random.fold_in(streams_of[6], part), 7)
    tokens = draw_tokens(jax.random.fold_in(jax.random.fold_in(streams_of[6], part), 71), part)
    cotangent = bell_draw_with(part_keys[1], (BLOCKS, BLOCK, D), 1.0, 6.0, ((0, 16),), (0, 2, 16, 2.0))
    block_lang = draw_block_lang(jax.random.fold_in(jax.random.fold_in(streams_of[6], part), 71), part)
    gain = jnp.clip(1.0 + 0.18 * jax.random.normal(streams_of[3], (D,), jnp.float32), 0.1, 1.9)
    w_down = noise(streams_of[4], (D, LANGS * R), D ** -0.5, 0.09375, ((1, 16),))
    w_up = noise(streams_of[5], (LANGS * R, D), R ** -0.5, 0.1875, ((0, 16),))
    return {"tokens": tokens, "cotangent": cotangent, "block_lang": block_lang, "gain": gain, "w_down": w_down, "w_up": w_up}


EPSILON = 1e-06

def gelu_tanh(values):
    return jax.nn.gelu(values, approximate=True)

def reference(tokens, cotangent, block_lang, gain, w_down, w_up):
    slice_width = R // OWN
    grad_scale = 1.0 / math.sqrt(TOKENS)

    def one_block(carried, inputs):
        sum_down, sum_up, sum_gain = carried
        block_rows, block_cot, language = inputs
        wide_rows = block_rows.astype(jnp.float32)
        root_mean = jnp.sqrt(lax.optimization_barrier(jnp.mean(wide_rows * wide_rows, axis=-1, keepdims=True)) + EPSILON)
        unit_rows = wide_rows / root_mean
        normed = (unit_rows * gain).astype(jnp.bfloat16)
        offset = (language * R).astype(jnp.int32)
        down_block = lax.dynamic_slice_in_dim(w_down, offset, R, 1)
        up_block = lax.dynamic_slice_in_dim(w_up, offset, R, 0)
        preact = jnp.dot(normed, down_block, preferred_element_type=jnp.float32)
        activ_wide, pullback = jax.vjp(gelu_tanh, preact)
        activation = activ_wide.astype(jnp.bfloat16)
        upstream = jnp.dot(block_cot, up_block.T, preferred_element_type=jnp.float32)
        dpreact = pullback(upstream)[0].astype(jnp.bfloat16)
        branch = jnp.zeros(wide_rows.shape, jnp.float32)
        dnormed = jnp.zeros(wide_rows.shape, jnp.float32)
        for owner_index in range(OWN):
            begin_at = owner_index * slice_width
            end_at = begin_at + slice_width
            partial_out = jnp.dot(activation[:, begin_at:end_at], up_block[begin_at:end_at], preferred_element_type=jnp.float32)
            branch = branch + lax.optimization_barrier(partial_out.astype(jnp.bfloat16)).astype(jnp.float32)
            partial_back = jnp.dot(dpreact[:, begin_at:end_at], down_block[:, begin_at:end_at].T, preferred_element_type=jnp.float32)
            dnormed = dnormed + lax.optimization_barrier(partial_back.astype(jnp.bfloat16)).astype(jnp.float32)
        adapted = (wide_rows + branch).astype(jnp.bfloat16)
        up_term = jnp.dot(activation.T, block_cot, preferred_element_type=jnp.float32)
        down_term = jnp.dot(normed.T, dpreact, preferred_element_type=jnp.float32)
        sum_down = lax.dynamic_update_slice_in_dim(sum_down, lax.dynamic_slice_in_dim(sum_down, offset, R, 1) + down_term, offset, 1)
        sum_up = lax.dynamic_update_slice_in_dim(sum_up, lax.dynamic_slice_in_dim(sum_up, offset, R, 0) + up_term, offset, 0)
        sum_gain = sum_gain + lax.optimization_barrier(jnp.sum(dnormed * unit_rows, axis=0))
        scaled = dnormed * gain
        inner = lax.optimization_barrier(jnp.mean(scaled * unit_rows, axis=-1, keepdims=True))
        x_grad = (block_cot.astype(jnp.float32) + (scaled - unit_rows * inner) / root_mean).astype(jnp.bfloat16)
        return ((sum_down, sum_up, sum_gain), (adapted, x_grad))
    initial = (jnp.zeros((D, LANGS * R), jnp.float32), jnp.zeros((LANGS * R, D), jnp.float32), jnp.zeros((D,), jnp.float32))
    totals, results = lax.scan(one_block, initial, (tokens, cotangent, block_lang))
    sum_down, sum_up, sum_gain = totals
    adapted, x_grad = results
    return (adapted, x_grad, (sum_down * grad_scale).astype(jnp.bfloat16), (sum_up * grad_scale).astype(jnp.bfloat16), sum_gain * grad_scale)
```

```python
import functools
import math

import jax
import jax.numpy as jnp
from jax import lax
from jax.experimental import pallas as pl
from jax.experimental.pallas import tpu as pltpu
from jax.sharding import PartitionSpec as P

OWN = 4
MOSTB = 6
EPSILON = 1e-06
ANY = pl.BlockSpec(memory_space=pl.ANY)


def gelu_tanh(values):
    return jax.nn.gelu(values, approximate=True)


def route_tables(block_lang, languages):
    block_count = block_lang.shape[0]
    onehot = (block_lang[:, None] == jnp.arange(languages, dtype=jnp.int32)[None, :]).astype(
        jnp.int32
    )
    earlier = jnp.cumsum(onehot, axis=0) - onehot
    ranks = jnp.sum(earlier * onehot, axis=1)
    counts = jnp.sum(onehot, axis=0)
    places = jnp.arange(MOSTB, dtype=jnp.int32)
    matches = onehot[:, :, None] * (ranks[:, None, None] == places[None, None, :]).astype(jnp.int32)
    table = jnp.sum(matches * jnp.arange(block_count, dtype=jnp.int32)[:, None, None], axis=0)
    filled = places[None, :] < counts[:, None]
    return (ranks, table, filled)


def peer_of(kind, me, step, devices):
    if kind == "all":
        return lax.rem(me + step, devices)
    if kind == "across":
        return lax.rem(me + step * OWN, devices)
    return (me // OWN) * OWN + lax.rem(lax.rem(me, OWN) + step, OWN)


def size_of(kind, devices):
    return {"all": devices, "across": devices // OWN, "owners": OWN}[kind]


def exchange_kernel(devices, plans, n_in, n_out, *refs):
    ins, outs = refs[:n_in], refs[n_in : n_in + n_out]
    sems = refs[n_in + n_out :]
    me = lax.axis_index("fsdp")
    barrier = pltpu.get_barrier_semaphore()
    total = 0
    for kind, _ in plans:

        def greet(step, carry, kind=kind):
            pl.semaphore_signal(
                barrier,
                inc=1,
                device_id={"fsdp": peer_of(kind, me, step, devices)},
                device_id_type=pl.DeviceIdType.MESH,
            )
            return carry

        lax.fori_loop(1, size_of(kind, devices), greet, 0)
        total += size_of(kind, devices) - 1
    pl.semaphore_wait(barrier, total)

    def remote(at, index, step):
        kind, moves = plans[at]
        send, recv, _ = sems[3 * at : 3 * at + 3]
        source, take, target, put = moves[index]
        peer = peer_of(kind, me, step, devices)
        return pltpu.make_async_remote_copy(
            src_ref=take(ins[source], peer),
            dst_ref=put(outs[target], me),
            send_sem=send.at[index, step],
            recv_sem=recv.at[index, step],
            device_id={"fsdp": peer},
            device_id_type=pl.DeviceIdType.MESH,
        )

    def local(at, index):
        source, take, target, put = plans[at][1][index]
        own = sems[3 * at + 2]
        return pltpu.make_async_copy(take(ins[source], me), put(outs[target], me), own.at[index])

    for at, (kind, moves) in enumerate(plans):

        def begin(step, carry, at=at, moves=moves):
            for index in range(len(moves)):
                remote(at, index, step).start()
            return carry

        lax.fori_loop(1, size_of(kind, devices), begin, 0)
        for index in range(len(moves)):
            local(at, index).start()
    for at, (kind, moves) in enumerate(plans):

        def finish(step, carry, at=at, moves=moves):
            for index in range(len(moves)):
                remote(at, index, step).wait()
            return carry

        lax.fori_loop(1, size_of(kind, devices), finish, 0)
        for index in range(len(moves)):
            local(at, index).wait()


def exchange(devices, collective_id, plans, inputs, out_shapes):
    scratch = []
    for kind, moves in plans:
        count = size_of(kind, devices)
        scratch += [
            pltpu.SemaphoreType.DMA((len(moves), count)),
            pltpu.SemaphoreType.DMA((len(moves), count)),
            pltpu.SemaphoreType.DMA((len(moves),)),
        ]
    return pl.pallas_call(
        functools.partial(exchange_kernel, devices, plans, len(inputs), len(out_shapes)),
        out_shape=[jax.ShapeDtypeStruct(shape, dtype) for shape, dtype in out_shapes],
        in_specs=[ANY] * len(inputs),
        out_specs=[ANY] * len(out_shapes),
        scratch_shapes=scratch,
        compiler_params=pltpu.CompilerParams(
            collective_id=collective_id, has_side_effects=True
        ),
    )(*inputs)


def span(index, width):
    return pl.ds(pl.multiple_of(index * width, width), width)


def per_device(tokens, cotangent, block_lang, gain, w_down, w_up):
    bf16, f32 = jnp.bfloat16, jnp.float32
    devices = lax.axis_size("fsdp")
    languages = devices // OWN
    per_block, width = tokens.shape[1:]
    rows = per_block // languages
    quarter = width // OWN
    units = w_down.shape[1]
    hidden = units * OWN
    gain_width = gain.shape[0]
    slots = languages * MOSTB * rows
    grad_scale = 1.0 / math.sqrt(devices * per_block)
    me = lax.axis_index("fsdp")
    rank_here = lax.rem(me, OWN)

    ranks, table, filled = route_tables(block_lang, languages)
    home = tokens.reshape(per_block, width).astype(f32)
    home_cot = cotangent.reshape(per_block, width)
    root_mean = jnp.sqrt(jnp.mean(home * home, axis=-1, keepdims=True) + EPSILON)

    def slab(ref, peer):
        return ref.at[peer // OWN, :, span(lax.rem(peer, OWN), quarter)]

    def whole(ref, peer):
        return ref.at[0]

    def piece(ref, peer):
        return ref.at[peer // OWN]

    def at_device(ref, me):
        return ref.at[me]

    spread_tok, spread_cot, spread_root, gain_all = exchange(
        devices,
        1,
        [
            (
                "all",
                [
                    (2, piece, 2, at_device),
                    (3, whole, 3, at_device),
                    (0, slab, 0, at_device),
                    (1, slab, 1, at_device),
                ],
            )
        ],
        [
            tokens.reshape(languages, rows, width),
            cotangent.reshape(languages, rows, width),
            jnp.broadcast_to(root_mean, (per_block, 128)).reshape(languages, rows, 128),
            jnp.broadcast_to(gain, (1, 8, gain_width)),
        ],
        [
            ((devices, rows, quarter), bf16),
            ((devices, rows, quarter), bf16),
            ((devices, rows, 128), f32),
            ((devices, 8, gain_width), f32),
        ],
    )
    gain_full = gain_all[:, 0, :].reshape(width)
    gain_here = lax.dynamic_slice_in_dim(gain_full, rank_here * quarter, quarter)
    unit_rows = spread_tok.astype(f32) / spread_root[:, :, :1]
    normed = (unit_rows * gain_here).astype(bf16)

    def pick(values):
        return jnp.where(filled[:, :, None, None], values[table], jnp.zeros((), bf16))

    def at_place(ref, me):
        return ref.at[me // OWN]

    rows_in, cot_in, down, up = exchange(
        devices,
        2,
        [
            ("across", [(0, piece, 0, at_place), (1, piece, 1, at_place)]),
            (
                "owners",
                [
                    (
                        2,
                        lambda ref, peer: ref.at[span(lax.rem(peer, OWN), quarter), :],
                        2,
                        lambda ref, me: ref.at[:, span(lax.rem(me, OWN), units)],
                    ),
                    (
                        3,
                        lambda ref, peer: ref.at[:, span(lax.rem(peer, OWN), quarter)],
                        3,
                        lambda ref, me: ref.at[span(lax.rem(me, OWN), units), :],
                    ),
                ],
            ),
        ],
        [pick(normed), pick(spread_cot), w_down, w_up],
        [
            ((languages, MOSTB, rows, quarter), bf16),
            ((languages, MOSTB, rows, quarter), bf16),
            ((quarter, hidden), bf16),
            ((hidden, quarter), bf16),
        ],
    )
    rows_in = rows_in.reshape(slots, quarter)
    cot_in = cot_in.reshape(slots, quarter)

    part_pre = jnp.dot(rows_in, down, preferred_element_type=f32).astype(bf16)
    part_up = jnp.dot(cot_in, up.T, preferred_element_type=f32).astype(bf16)

    def unit_span(ref, peer):
        return ref.at[:, span(lax.rem(peer, OWN), units)]

    def at_rank(ref, me):
        return ref.at[lax.rem(me, OWN)]

    pre_parts, up_parts = exchange(
        devices,
        3,
        [("owners", [(0, unit_span, 0, at_rank), (1, unit_span, 1, at_rank)])],
        [part_pre, part_up],
        [((OWN, slots, units), bf16), ((OWN, slots, units), bf16)],
    )
    preact = jnp.sum(pre_parts, axis=0, dtype=f32)
    upstream = jnp.sum(up_parts, axis=0, dtype=f32)
    activ_wide, pullback = jax.vjp(gelu_tanh, preact)
    dpreact_here = pullback(upstream)[0].astype(bf16)

    def all_of(ref, peer):
        return ref

    activation, dpreact = exchange(
        devices,
        4,
        [("owners", [(0, all_of, 0, unit_span), (1, all_of, 1, unit_span)])],
        [activ_wide.astype(bf16), dpreact_here],
        [((slots, hidden), bf16), ((slots, hidden), bf16)],
    )
    shape = (languages, MOSTB, rows, quarter)
    out = jnp.dot(activation, up, preferred_element_type=f32).astype(bf16).reshape(shape)
    back = jnp.dot(dpreact, down.T, preferred_element_type=f32).astype(bf16).reshape(shape)
    part_grad_up = (
        jnp.dot(activation.T, cot_in, preferred_element_type=f32) * grad_scale
    ).astype(bf16)
    part_grad_down = (
        jnp.dot(rows_in.T, dpreact, preferred_element_type=f32) * grad_scale
    ).astype(bf16)

    out_home, back_home, grad_down, grad_up = exchange(
        devices,
        5,
        [
            ("across", [(0, piece, 0, at_place), (1, piece, 1, at_place)]),
            (
                "owners",
                [
                    (
                        2,
                        unit_span,
                        2,
                        lambda ref, me: ref.at[span(lax.rem(me, OWN), quarter), :],
                    ),
                    (
                        3,
                        lambda ref, peer: ref.at[span(lax.rem(peer, OWN), units), :],
                        3,
                        lambda ref, me: ref.at[:, span(lax.rem(me, OWN), quarter)],
                    ),
                ],
            ),
        ],
        [out, back, part_grad_down, part_grad_up],
        [(shape, bf16), (shape, bf16), ((width, units), bf16), ((units, width), bf16)],
    )
    branch_rows = out_home[block_lang, ranks]
    dnormed_rows = back_home[block_lang, ranks]
    gain_part = jnp.sum(dnormed_rows.astype(f32) * unit_rows, axis=(0, 1))

    def at_home(ref, me):
        return ref.at[me // OWN, :, span(lax.rem(me, OWN), quarter)]

    branch, dnormed, gain_parts = exchange(
        devices,
        6,
        [
            (
                "all",
                [
                    (2, lambda ref, peer: ref.at[lax.rem(peer, languages)], 2, at_device),
                    (0, at_device, 0, at_home),
                    (1, at_device, 1, at_home),
                ],
            )
        ],
        [
            branch_rows,
            dnormed_rows,
            jnp.broadcast_to(
                gain_part.reshape(languages, 1, gain_width), (languages, 8, gain_width)
            ),
        ],
        [
            ((languages, rows, width), bf16),
            ((languages, rows, width), bf16),
            ((devices, 8, gain_width), f32),
        ],
    )
    holders = gain_parts[:, 0, :].reshape(languages, OWN, gain_width)
    grad_gain = (
        jnp.sum(
            lax.dynamic_index_in_dim(holders, me // languages, axis=1, keepdims=False), axis=0
        )
        * grad_scale
    )
    adapted = (home + branch.reshape(per_block, width).astype(f32)).astype(bf16)
    unit = home / root_mean
    scaled = dnormed.reshape(per_block, width).astype(f32) * gain_full
    inner = jnp.mean(scaled * unit, axis=-1, keepdims=True)
    x_grad = (home_cot.astype(f32) + (scaled - unit * inner) / root_mean).astype(bf16)
    return (
        adapted.reshape(tokens.shape),
        x_grad.reshape(tokens.shape),
        grad_down,
        grad_up,
        grad_gain,
    )


def solution(mesh):
    in_specs = (
        P(("groups", "fsdp"), None, None),
        P(("groups", "fsdp"), None, None),
        P("groups"),
        P("fsdp"),
        P(None, "fsdp"),
        P("fsdp", None),
    )
    out_specs = (
        P(("groups", "fsdp"), None, None),
        P(("groups", "fsdp"), None, None),
        P("groups", "fsdp"),
        P(("groups", "fsdp"), None),
        P(("groups", "fsdp")),
    )
    return jax.shard_map(
        per_device, mesh=mesh, in_specs=in_specs, out_specs=out_specs, check_vma=False
    )
```

```python
import functools
import math

import jax
import jax.numpy as jnp
from jax import lax
from jax.experimental import pallas as pl
from jax.experimental.pallas import tpu as pltpu
from jax.sharding import PartitionSpec as P

OWN = 4
MOSTB = 6
EPSILON = 1e-06
ANY = pl.BlockSpec(memory_space=pl.ANY)


def gelu_tanh(values):
    return jax.nn.gelu(values, approximate=True)


def route_tables(block_lang, languages):
    block_count = block_lang.shape[0]
    onehot = (block_lang[:, None] == jnp.arange(languages, dtype=jnp.int32)[None, :]).astype(
        jnp.int32
    )
    earlier = jnp.cumsum(onehot, axis=0) - onehot
    ranks = jnp.sum(earlier * onehot, axis=1)
    counts = jnp.sum(onehot, axis=0)
    places = jnp.arange(MOSTB, dtype=jnp.int32)
    matches = onehot[:, :, None] * (ranks[:, None, None] == places[None, None, :]).astype(jnp.int32)
    table = jnp.sum(matches * jnp.arange(block_count, dtype=jnp.int32)[:, None, None], axis=0)
    filled = places[None, :] < counts[:, None]
    return (ranks, table, filled)


def peer_of(kind, me, step, devices):
    if kind == "all":
        return lax.rem(me + step, devices)
    if kind == "across":
        return lax.rem(me + step * OWN, devices)
    return (me // OWN) * OWN + lax.rem(lax.rem(me, OWN) + step, OWN)


def size_of(kind, devices):
    return {"all": devices, "across": devices // OWN, "owners": OWN}[kind]


def exchange_kernel(devices, plans, n_in, n_out, *refs):
    ins, outs = refs[:n_in], refs[n_in : n_in + n_out]
    sems = refs[n_in + n_out :]
    me = lax.axis_index("fsdp")
    barrier = pltpu.get_barrier_semaphore()
    total = 0
    for kind, _ in plans:

        def greet(step, carry, kind=kind):
            pl.semaphore_signal(
                barrier,
                inc=1,
                device_id={"fsdp": peer_of(kind, me, step, devices)},
                device_id_type=pl.DeviceIdType.MESH,
            )
            return carry

        lax.fori_loop(1, size_of(kind, devices), greet, 0)
        total += size_of(kind, devices) - 1
    pl.semaphore_wait(barrier, total)

    def remote(at, index, step):
        kind, moves = plans[at]
        send, recv, _ = sems[3 * at : 3 * at + 3]
        source, take, target, put = moves[index]
        peer = peer_of(kind, me, step, devices)
        return pltpu.make_async_remote_copy(
            src_ref=take(ins[source], peer),
            dst_ref=put(outs[target], me),
            send_sem=send.at[index, step],
            recv_sem=recv.at[index, step],
            device_id={"fsdp": peer},
            device_id_type=pl.DeviceIdType.MESH,
        )

    def local(at, index):
        source, take, target, put = plans[at][1][index]
        own = sems[3 * at + 2]
        return pltpu.make_async_copy(take(ins[source], me), put(outs[target], me), own.at[index])

    for at, (kind, moves) in enumerate(plans):

        def begin(step, carry, at=at, moves=moves):
            for index in range(len(moves)):
                remote(at, index, step).start()
            return carry

        lax.fori_loop(1, size_of(kind, devices), begin, 0)
        for index in range(len(moves)):
            local(at, index).start()
    for at, (kind, moves) in enumerate(plans):

        def finish(step, carry, at=at, moves=moves):
            for index in range(len(moves)):
                remote(at, index, step).wait()
            return carry

        lax.fori_loop(1, size_of(kind, devices), finish, 0)
        for index in range(len(moves)):
            local(at, index).wait()


def exchange(devices, collective_id, plans, inputs, out_shapes):
    scratch = []
    for kind, moves in plans:
        count = size_of(kind, devices)
        scratch += [
            pltpu.SemaphoreType.DMA((len(moves), count)),
            pltpu.SemaphoreType.DMA((len(moves), count)),
            pltpu.SemaphoreType.DMA((len(moves),)),
        ]
    return pl.pallas_call(
        functools.partial(exchange_kernel, devices, plans, len(inputs), len(out_shapes)),
        out_shape=[jax.ShapeDtypeStruct(shape, dtype) for shape, dtype in out_shapes],
        in_specs=[ANY] * len(inputs),
        out_specs=[ANY] * len(out_shapes),
        scratch_shapes=scratch,
        compiler_params=pltpu.CompilerParams(
            collective_id=collective_id, has_side_effects=True
        ),
    )(*inputs)


def span(index, width):
    return pl.ds(pl.multiple_of(index * width, width), width)


ROW_TILE = 256
TRANSFERS = 12
TOK, COT, DOWN, UP, PRE, UPS, ACT, DPRE, OUT, BACK, GUP, GDOWN = range(TRANSFERS)
GELU_C = math.sqrt(2.0 / math.pi)


def adapter_kernel(
    devices, grad_scale, tok_ref, cot_ref, wd_ref, wu_ref, out_ref, back_ref, gd_ref, gu_ref,
    rows, cots, down, up, pre_out, pre_in, ups_out, ups_in, act, dpre, slope, out, back, gup, gdown,
    send, recv, own,
):
    bf16, f32 = jnp.bfloat16, jnp.float32
    me = lax.axis_index("fsdp")
    group, rank = me // OWN, lax.rem(me, OWN)
    languages = devices // OWN
    slots, quarter = rows.shape
    chunk = slots // languages
    units = wd_ref.shape[1]
    wide = min(512, quarter)
    tiles = slots // ROW_TILE

    barrier = pltpu.get_barrier_semaphore()
    for kind in ("across", "owners"):

        def greet(step, carry, kind=kind):
            pl.semaphore_signal(
                barrier,
                inc=1,
                device_id={"fsdp": peer_of(kind, me, step, devices)},
                device_id_type=pl.DeviceIdType.MESH,
            )
            return carry

        lax.fori_loop(1, size_of(kind, devices), greet, 0)
    pl.semaphore_wait(barrier, languages - 1 + OWN - 1)

    def group_rows(ref):
        return lambda device, step: ref.at[span(device // OWN, chunk), :]

    def feature_rows(ref):
        return lambda device, step: ref.at[span(lax.rem(device, OWN), quarter), :]

    def feature_columns(ref):
        return lambda device, step: ref.at[:, span(lax.rem(device, OWN), quarter)]

    def unit_rows(ref):
        return lambda device, step: ref.at[span(lax.rem(device, OWN), units), :]

    def unit_columns(ref):
        return lambda device, step: ref.at[:, span(lax.rem(device, OWN), units)]

    def by_rank(ref):
        return lambda device, step: ref.at[lax.rem(device, OWN)]

    def by_step(ref):
        return lambda device, step: ref.at[step - 1]

    def mine(ref):
        return lambda device, step: ref.at[rank]

    moves = {
        TOK: ("across", group_rows(tok_ref), group_rows(rows), True),
        COT: ("across", group_rows(cot_ref), group_rows(cots), True),
        DOWN: ("owners", feature_rows(wd_ref), unit_columns(down), True),
        UP: ("owners", feature_columns(wu_ref), unit_rows(up), True),
        PRE: ("owners", by_rank(pre_out), by_step(pre_in), False),
        UPS: ("owners", by_rank(ups_out), by_step(ups_in), False),
        ACT: ("owners", mine(act), mine(act), False),
        DPRE: ("owners", mine(dpre), mine(dpre), False),
        OUT: ("across", group_rows(out), group_rows(out_ref), True),
        BACK: ("across", group_rows(back), group_rows(back_ref), True),
        GUP: ("owners", by_rank(gup), feature_columns(gu_ref), True),
        GDOWN: ("owners", by_rank(gdown), feature_rows(gd_ref), True),
    }

    def remote(name, step):
        kind, take, put, _ = moves[name]
        peer = peer_of(kind, me, step, devices)
        return pltpu.make_async_remote_copy(
            src_ref=take(peer, step),
            dst_ref=put(me, step),
            send_sem=send.at[name, step],
            recv_sem=recv.at[name, step],
            device_id={"fsdp": peer},
            device_id_type=pl.DeviceIdType.MESH,
        )

    def local(name):
        _, take, put, _ = moves[name]
        return pltpu.make_async_copy(take(me, 0), put(me, 0), own.at[name])

    def begin(name):
        def body(step, carry):
            remote(name, step).start()
            return carry

        lax.fori_loop(1, size_of(moves[name][0], devices), body, 0)
        if moves[name][3]:
            local(name).start()

    def finish(name):
        def body(step, carry):
            remote(name, step).wait()
            return carry

        lax.fori_loop(1, size_of(moves[name][0], devices), body, 0)
        if moves[name][3]:
            local(name).wait()

    def dot(left, right, over):
        return lax.dot_general(left, right, ((over[:1], over[1:]), ((), ())), preferred_element_type=f32)

    def each(count, body):
        def wrapped(index, carry):
            body(index)
            return carry

        lax.fori_loop(0, count, wrapped, 0)

    def gathered(ref, at):
        return jnp.concatenate([ref[owner, at, :] for owner in range(OWN)], axis=1)

    begin(TOK)
    begin(DOWN)
    finish(TOK)
    finish(DOWN)
    begin(COT)
    begin(UP)

    def pre_tile(index):
        at = span(index, ROW_TILE)
        block = rows[at, :]
        for owner in range(OWN):
            columns = pl.ds(owner * units, units)
            pre_out[owner, at, :] = dot(block, down[:, columns], (1, 0)).astype(bf16)

    each(tiles, pre_tile)
    begin(PRE)
    finish(PRE)

    def act_tile(index):
        at = span(index, ROW_TILE)
        value = pre_out[rank, at, :].astype(f32)
        for step in range(OWN - 1):
            value = value + pre_in[step, at, :].astype(f32)
        square = value * value
        bent = jnp.tanh(GELU_C * (value + 0.044715 * (square * value)))
        half = 0.5 * (1.0 + bent)
        act[rank, at, :] = (value * half).astype(bf16)
        slope[at, :] = half + (0.5 * GELU_C) * value * (1.0 - bent * bent) * (
            1.0 + (3.0 * 0.044715) * square
        )

    each(tiles, act_tile)
    begin(ACT)
    finish(COT)
    finish(UP)

    def ups_tile(index):
        at = span(index, ROW_TILE)
        block = cots[at, :]
        for owner in range(OWN):
            ups_out[owner, at, :] = dot(block, up[pl.ds(owner * units, units), :], (1, 1)).astype(
                bf16
            )

    each(tiles, ups_tile)
    finish(ACT)
    begin(UPS)

    def out_tile(index):
        at = span(index, ROW_TILE)
        block = gathered(act, at)
        for first in range(0, quarter, wide):
            columns = pl.ds(first, wide)
            out[at, columns] = dot(block, up[:, columns], (1, 0)).astype(bf16)

    each(tiles, out_tile)
    begin(OUT)
    finish(UPS)

    def dpre_tile(index):
        at = span(index, ROW_TILE)
        value = ups_out[rank, at, :].astype(f32)
        for step in range(OWN - 1):
            value = value + ups_in[step, at, :].astype(f32)
        dpre[rank, at, :] = (slope[at, :] * value).astype(bf16)

    each(tiles, dpre_tile)
    begin(DPRE)

    def gup_tile(owner):
        left = act[owner]
        for first in range(0, quarter, wide):
            columns = pl.ds(first, wide)
            gup[owner, :, columns] = (dot(left, cots[:, columns], (0, 0)) * grad_scale).astype(bf16)

    each(OWN, gup_tile)
    finish(DPRE)
    begin(GUP)

    def back_tile(index):
        at = span(index, ROW_TILE)
        block = gathered(dpre, at)
        for first in range(0, quarter, wide):
            columns = pl.ds(first, wide)
            back[at, columns] = dot(block, down[columns, :], (1, 1)).astype(bf16)

    each(tiles, back_tile)
    begin(BACK)

    def gdown_tile(owner):
        right = dpre[owner]
        for first in range(0, quarter, wide):
            columns = pl.ds(first, wide)
            gdown[owner, columns, :] = (dot(rows[:, columns], right, (0, 0)) * grad_scale).astype(
                bf16
            )

    each(OWN, gdown_tile)
    begin(GDOWN)
    for name in (GUP, OUT, GDOWN, BACK):
        finish(name)


def adapter(devices, grad_scale, tok, cot, w_down, w_up):
    bf16 = jnp.bfloat16
    slots, quarter = tok.shape
    width, units = w_down.shape
    hidden = units * OWN
    steps = max(devices // OWN, OWN)
    whole = pltpu.VMEM((OWN, slots, units), bf16)
    received = pltpu.VMEM((OWN - 1, slots, units), bf16)
    wide_rows = pltpu.VMEM((slots, quarter), bf16)
    return pl.pallas_call(
        functools.partial(adapter_kernel, devices, grad_scale),
        out_shape=[
            jax.ShapeDtypeStruct((slots, quarter), bf16),
            jax.ShapeDtypeStruct((slots, quarter), bf16),
            jax.ShapeDtypeStruct((width, units), bf16),
            jax.ShapeDtypeStruct((units, width), bf16),
        ],
        in_specs=[ANY] * 4,
        out_specs=[ANY] * 4,
        scratch_shapes=[
            wide_rows,
            wide_rows,
            pltpu.VMEM((quarter, hidden), bf16),
            pltpu.VMEM((hidden, quarter), bf16),
            whole,
            received,
            whole,
            received,
            whole,
            whole,
            pltpu.VMEM((slots, units), jnp.float32),
            wide_rows,
            wide_rows,
            pltpu.VMEM((OWN, units, quarter), bf16),
            pltpu.VMEM((OWN, quarter, units), bf16),
            pltpu.SemaphoreType.DMA((TRANSFERS, steps)),
            pltpu.SemaphoreType.DMA((TRANSFERS, steps)),
            pltpu.SemaphoreType.DMA((TRANSFERS,)),
        ],
        compiler_params=pltpu.CompilerParams(
            collective_id=2, has_side_effects=True, vmem_limit_bytes=48 * 1024 * 1024
        ),
    )(tok, cot, w_down, w_up)


def per_device(tokens, cotangent, block_lang, gain, w_down, w_up):
    bf16, f32 = jnp.bfloat16, jnp.float32
    devices = lax.axis_size("fsdp")
    languages = devices // OWN
    per_block, width = tokens.shape[1:]
    rows = per_block // languages
    quarter = width // OWN
    units = w_down.shape[1]
    hidden = units * OWN
    gain_width = gain.shape[0]
    slots = languages * MOSTB * rows
    grad_scale = 1.0 / math.sqrt(devices * per_block)
    me = lax.axis_index("fsdp")
    rank_here = lax.rem(me, OWN)

    ranks, table, filled = route_tables(block_lang, languages)
    home = tokens.reshape(per_block, width).astype(f32)
    home_cot = cotangent.reshape(per_block, width)
    root_mean = jnp.sqrt(jnp.mean(home * home, axis=-1, keepdims=True) + EPSILON)

    def slab(ref, peer):
        return ref.at[peer // OWN, :, span(lax.rem(peer, OWN), quarter)]

    def whole(ref, peer):
        return ref.at[0]

    def piece(ref, peer):
        return ref.at[peer // OWN]

    def at_device(ref, me):
        return ref.at[me]

    spread_tok, spread_cot, spread_root, gain_all = exchange(
        devices,
        1,
        [
            (
                "all",
                [
                    (2, piece, 2, at_device),
                    (3, whole, 3, at_device),
                    (0, slab, 0, at_device),
                    (1, slab, 1, at_device),
                ],
            )
        ],
        [
            tokens.reshape(languages, rows, width),
            cotangent.reshape(languages, rows, width),
            jnp.broadcast_to(root_mean, (per_block, 128)).reshape(languages, rows, 128),
            jnp.broadcast_to(gain, (1, 8, gain_width)),
        ],
        [
            ((devices, rows, quarter), bf16),
            ((devices, rows, quarter), bf16),
            ((devices, rows, 128), f32),
            ((devices, 8, gain_width), f32),
        ],
    )
    gain_full = gain_all[:, 0, :].reshape(width)
    gain_here = lax.dynamic_slice_in_dim(gain_full, rank_here * quarter, quarter)
    unit_rows = spread_tok.astype(f32) / spread_root[:, :, :1]
    normed = (unit_rows * gain_here).astype(bf16)

    def pick(values):
        return jnp.where(filled[:, :, None, None], values[table], jnp.zeros((), bf16))

    chunk = -(-MOSTB * rows // 16) * 16

    def packed(values):
        picked = pick(values).reshape(languages, MOSTB * rows, quarter)
        filler = ((0, 0), (0, chunk - MOSTB * rows), (0, 0))
        return jnp.pad(picked, filler).reshape(languages * chunk, quarter)

    def unpacked(values):
        shaped = values.reshape(languages, chunk, quarter)[:, : MOSTB * rows]
        return shaped.reshape(languages, MOSTB, rows, quarter)

    out_home, back_home, grad_down, grad_up = adapter(
        devices, grad_scale, packed(normed), packed(spread_cot), w_down, w_up
    )
    out_home, back_home = unpacked(out_home), unpacked(back_home)
    branch_rows = out_home[block_lang, ranks]
    dnormed_rows = back_home[block_lang, ranks]
    gain_part = jnp.sum(dnormed_rows.astype(f32) * unit_rows, axis=(0, 1))

    def at_home(ref, me):
        return ref.at[me // OWN, :, span(lax.rem(me, OWN), quarter)]

    branch, dnormed, gain_parts = exchange(
        devices,
        3,
        [
            (
                "all",
                [
                    (2, lambda ref, peer: ref.at[lax.rem(peer, languages)], 2, at_device),
                    (0, at_device, 0, at_home),
                    (1, at_device, 1, at_home),
                ],
            )
        ],
        [
            branch_rows,
            dnormed_rows,
            jnp.broadcast_to(
                gain_part.reshape(languages, 1, gain_width), (languages, 8, gain_width)
            ),
        ],
        [
            ((languages, rows, width), bf16),
            ((languages, rows, width), bf16),
            ((devices, 8, gain_width), f32),
        ],
    )
    holders = gain_parts[:, 0, :].reshape(languages, OWN, gain_width)
    grad_gain = (
        jnp.sum(
            lax.dynamic_index_in_dim(holders, me // languages, axis=1, keepdims=False), axis=0
        )
        * grad_scale
    )
    adapted = (home + branch.reshape(per_block, width).astype(f32)).astype(bf16)
    unit = home / root_mean
    scaled = dnormed.reshape(per_block, width).astype(f32) * gain_full
    inner = jnp.mean(scaled * unit, axis=-1, keepdims=True)
    x_grad = (home_cot.astype(f32) + (scaled - unit * inner) / root_mean).astype(bf16)
    return (
        adapted.reshape(tokens.shape),
        x_grad.reshape(tokens.shape),
        grad_down,
        grad_up,
        grad_gain,
    )


def solution(mesh):
    in_specs = (
        P(("groups", "fsdp"), None, None),
        P(("groups", "fsdp"), None, None),
        P("groups"),
        P("fsdp"),
        P(None, "fsdp"),
        P("fsdp", None),
    )
    out_specs = (
        P(("groups", "fsdp"), None, None),
        P(("groups", "fsdp"), None, None),
        P("groups", "fsdp"),
        P(("groups", "fsdp"), None),
        P(("groups", "fsdp")),
    )
    return jax.shard_map(
        per_device, mesh=mesh, in_specs=in_specs, out_specs=out_specs, check_vma=False
    )
```

```python
import functools
import math

import jax
import jax.numpy as jnp
from jax import lax
from jax.experimental import pallas as pl
from jax.experimental.pallas import tpu as pltpu
from jax.sharding import PartitionSpec as P

OWN = 4
MOSTB = 6
EPSILON = 1e-06
ANY = pl.BlockSpec(memory_space=pl.ANY)


def gelu_tanh(values):
    return jax.nn.gelu(values, approximate=True)


def route_tables(block_lang, languages):
    block_count = block_lang.shape[0]
    onehot = (block_lang[:, None] == jnp.arange(languages, dtype=jnp.int32)[None, :]).astype(
        jnp.int32
    )
    earlier = jnp.cumsum(onehot, axis=0) - onehot
    ranks = jnp.sum(earlier * onehot, axis=1)
    counts = jnp.sum(onehot, axis=0)
    places = jnp.arange(MOSTB, dtype=jnp.int32)
    matches = onehot[:, :, None] * (ranks[:, None, None] == places[None, None, :]).astype(jnp.int32)
    table = jnp.sum(matches * jnp.arange(block_count, dtype=jnp.int32)[:, None, None], axis=0)
    filled = places[None, :] < counts[:, None]
    return (ranks, table, filled)


def peer_of(kind, me, step, devices):
    if kind == "all":
        return lax.rem(me + step, devices)
    if kind == "across":
        return lax.rem(me + step * OWN, devices)
    return (me // OWN) * OWN + lax.rem(lax.rem(me, OWN) + step, OWN)


def size_of(kind, devices):
    return {"all": devices, "across": devices // OWN, "owners": OWN}[kind]


def exchange_kernel(devices, plans, n_in, n_out, *refs):
    ins, outs = refs[:n_in], refs[n_in : n_in + n_out]
    sems = refs[n_in + n_out :]
    me = lax.axis_index("fsdp")
    barrier = pltpu.get_barrier_semaphore()
    total = 0
    for kind, _ in plans:

        def greet(step, carry, kind=kind):
            pl.semaphore_signal(
                barrier,
                inc=1,
                device_id={"fsdp": peer_of(kind, me, step, devices)},
                device_id_type=pl.DeviceIdType.MESH,
            )
            return carry

        lax.fori_loop(1, size_of(kind, devices), greet, 0)
        total += size_of(kind, devices) - 1
    pl.semaphore_wait(barrier, total)

    def remote(at, index, step):
        kind, moves = plans[at]
        send, recv, _ = sems[3 * at : 3 * at + 3]
        source, take, target, put = moves[index]
        peer = peer_of(kind, me, step, devices)
        return pltpu.make_async_remote_copy(
            src_ref=take(ins[source], peer),
            dst_ref=put(outs[target], me),
            send_sem=send.at[index, step],
            recv_sem=recv.at[index, step],
            device_id={"fsdp": peer},
            device_id_type=pl.DeviceIdType.MESH,
        )

    def local(at, index):
        source, take, target, put = plans[at][1][index]
        own = sems[3 * at + 2]
        return pltpu.make_async_copy(take(ins[source], me), put(outs[target], me), own.at[index])

    for at, (kind, moves) in enumerate(plans):

        def begin(step, carry, at=at, moves=moves):
            for index in range(len(moves)):
                remote(at, index, step).start()
            return carry

        lax.fori_loop(1, size_of(kind, devices), begin, 0)
        for index in range(len(moves)):
            local(at, index).start()
    for at, (kind, moves) in enumerate(plans):

        def finish(step, carry, at=at, moves=moves):
            for index in range(len(moves)):
                remote(at, index, step).wait()
            return carry

        lax.fori_loop(1, size_of(kind, devices), finish, 0)
        for index in range(len(moves)):
            local(at, index).wait()


def exchange(devices, collective_id, plans, inputs, out_shapes):
    scratch = []
    for kind, moves in plans:
        count = size_of(kind, devices)
        scratch += [
            pltpu.SemaphoreType.DMA((len(moves), count)),
            pltpu.SemaphoreType.DMA((len(moves), count)),
            pltpu.SemaphoreType.DMA((len(moves),)),
        ]
    return pl.pallas_call(
        functools.partial(exchange_kernel, devices, plans, len(inputs), len(out_shapes)),
        out_shape=[jax.ShapeDtypeStruct(shape, dtype) for shape, dtype in out_shapes],
        in_specs=[ANY] * len(inputs),
        out_specs=[ANY] * len(out_shapes),
        scratch_shapes=scratch,
        compiler_params=pltpu.CompilerParams(
            collective_id=collective_id, has_side_effects=True
        ),
    )(*inputs)


def span(index, width):
    return pl.ds(pl.multiple_of(index * width, width), width)


ROW_TILE = 256
TRANSFERS = 12
TOK, COT, DOWN, UP, PRE, UPS, ACT, DPRE, OUT, BACK, GUP, GDOWN = range(TRANSFERS)
GELU_C = math.sqrt(2.0 / math.pi)


def adapter_kernel(
    devices, grad_scale, tok_ref, cot_ref, wd_ref, wu_ref, out_ref, back_ref, gd_ref, gu_ref,
    rows, cots, down, up, pre_out, pre_in, ups_out, ups_in, act, dpre, slope, out, back, gup, gdown,
    send, recv, own,
):
    bf16, f32 = jnp.bfloat16, jnp.float32
    me = lax.axis_index("fsdp")
    group, rank = me // OWN, lax.rem(me, OWN)
    languages = devices // OWN
    slots, quarter = rows.shape
    chunk = slots // languages
    units = wu_ref.shape[0]
    side, core = rank // 2, lax.rem(rank, 2)
    twin, facing, opposite = side * 2 + 1 - core, (1 - side) * 2 + core, (1 - side) * 2 + 1 - core
    wide = min(512, quarter)
    tiles = slots // ROW_TILE

    barrier = pltpu.get_barrier_semaphore()
    for kind in ("across", "owners"):

        def greet(step, carry, kind=kind):
            pl.semaphore_signal(
                barrier,
                inc=1,
                device_id={"fsdp": peer_of(kind, me, step, devices)},
                device_id_type=pl.DeviceIdType.MESH,
            )
            return carry

        lax.fori_loop(1, size_of(kind, devices), greet, 0)
    pl.semaphore_wait(barrier, languages - 1 + OWN - 1)

    def group_rows(ref):
        return lambda device, step: ref.at[span(device // OWN, chunk), :]

    def feature_rows(ref):
        return lambda device, step: ref.at[span(lax.rem(device, OWN), quarter), :]

    def feature_columns(ref):
        return lambda device, step: ref.at[:, span(lax.rem(device, OWN), quarter)]

    def unit_rows(ref):
        return lambda device, step: ref.at[span(lax.rem(device, OWN), units), :]

    def by_rank(ref):
        return lambda device, step: ref.at[lax.rem(device, OWN)]

    moves = {
        TOK: ("across", group_rows(tok_ref), group_rows(rows), True),
        COT: ("across", group_rows(cot_ref), group_rows(cots), True),
        UP: ("owners", feature_columns(wu_ref), unit_rows(up), True),
        OUT: ("across", group_rows(out), group_rows(out_ref), True),
        BACK: ("across", group_rows(back), group_rows(back_ref), True),
        GUP: ("owners", by_rank(gup), feature_columns(gu_ref), True),
        GDOWN: ("owners", by_rank(gdown), feature_rows(gd_ref), True),
    }

    def remote(name, step):
        kind, take, put, _ = moves[name]
        peer = peer_of(kind, me, step, devices)
        return pltpu.make_async_remote_copy(
            src_ref=take(peer, step),
            dst_ref=put(me, step),
            send_sem=send.at[name, step],
            recv_sem=recv.at[name, step],
            device_id={"fsdp": peer},
            device_id_type=pl.DeviceIdType.MESH,
        )

    def local(name):
        _, take, put, _ = moves[name]
        return pltpu.make_async_copy(take(me, 0), put(me, 0), own.at[name])

    def begin(name):
        def body(step, carry):
            remote(name, step).start()
            return carry

        lax.fori_loop(1, size_of(moves[name][0], devices), body, 0)
        if moves[name][3]:
            local(name).start()

    def finish(name):
        def body(step, carry):
            remote(name, step).wait()
            return carry

        lax.fori_loop(1, size_of(moves[name][0], devices), body, 0)
        if moves[name][3]:
            local(name).wait()

    def direct(name, slot, source, target, rank_to):
        return pltpu.make_async_remote_copy(
            src_ref=source,
            dst_ref=target,
            send_sem=send.at[name, slot],
            recv_sem=recv.at[name, slot],
            device_id={"fsdp": group * OWN + rank_to},
            device_id_type=pl.DeviceIdType.MESH,
        )

    def reduce(name, parts, landed, beside=None):
        final = direct(name, 1, parts.at[twin], landed.at[0], twin)
        paired = direct(name, 2, parts.at[opposite], landed.at[1], twin)
        paired.start()
        final.start()
        paired.wait()

        def pair_tile(index):
            at = span(index, ROW_TILE)
            both = parts[facing, at, :].astype(f32) + landed[1, at, :].astype(f32)
            parts[facing, at, :] = both.astype(bf16)

        each(tiles, pair_tile)
        crossing = direct(name, 3, parts.at[facing], landed.at[2], facing)
        crossing.start()
        if beside is not None:
            beside()
        final.wait()
        crossing.wait()

    def reduced(parts, landed, at):
        value = parts[rank, at, :].astype(f32) + landed[0, at, :].astype(f32)
        return value + landed[2, at, :].astype(f32)

    def gather(name, ref, beside=None):
        across = direct(name, 2, ref.at[rank], ref.at[rank], facing)
        beside_me = direct(name, 1, ref.at[rank], ref.at[rank], twin)
        across.start()
        beside_me.start()
        if beside is not None:
            beside()
        across.wait()
        passed = direct(name, 3, ref.at[facing], ref.at[facing], twin)
        passed.start()
        beside_me.wait()
        passed.wait()

    def dot(left, right, over):
        return lax.dot_general(left, right, ((over[:1], over[1:]), ((), ())), preferred_element_type=f32)

    def each(count, body):
        def wrapped(index, carry):
            body(index)
            return carry

        lax.fori_loop(0, count, wrapped, 0)

    def gathered(ref, at):
        return jnp.concatenate([ref[owner, at, :] for owner in range(OWN)], axis=1)

    begin(TOK)
    begin(UP)
    load_down = pltpu.make_async_copy(wd_ref, down, own.at[DOWN])
    load_down.start()
    load_down.wait()
    finish(TOK)
    begin(COT)

    def pre_tile(index):
        at = span(index, ROW_TILE)
        block = rows[at, :]
        for owner in range(OWN):
            columns = pl.ds(owner * units, units)
            pre_out[owner, at, :] = dot(block, down[:, columns], (1, 0)).astype(bf16)

    each(tiles, pre_tile)
    reduce(PRE, pre_out, pre_in)

    def act_tile(index):
        at = span(index, ROW_TILE)
        value = reduced(pre_out, pre_in, at)
        square = value * value
        bent = jnp.tanh(GELU_C * (value + 0.044715 * (square * value)))
        half = 0.5 * (1.0 + bent)
        act[rank, at, :] = (value * half).astype(bf16)
        slope[at, :] = half + (0.5 * GELU_C) * value * (1.0 - bent * bent) * (
            1.0 + (3.0 * 0.044715) * square
        )

    each(tiles, act_tile)
    gather(ACT, act)
    finish(UP)

    def out_tile(index):
        at = span(index, ROW_TILE)
        block = gathered(act, at)
        for first in range(0, quarter, wide):
            columns = pl.ds(first, wide)
            out[at, columns] = dot(block, up[:, columns], (1, 0)).astype(bf16)

    each(tiles, out_tile)
    begin(OUT)
    finish(COT)

    def ups_tile(index):
        at = span(index, ROW_TILE)
        block = cots[at, :]
        for owner in range(OWN):
            ups_out[owner, at, :] = dot(block, up[pl.ds(owner * units, units), :], (1, 1)).astype(
                bf16
            )

    each(tiles, ups_tile)

    def gup_tile(owner):
        left = act[owner]
        for first in range(0, quarter, wide):
            columns = pl.ds(first, wide)
            gup[owner, :, columns] = (dot(left, cots[:, columns], (0, 0)) * grad_scale).astype(bf16)

    reduce(UPS, ups_out, ups_in, lambda: each(OWN, gup_tile))

    def dpre_tile(index):
        at = span(index, ROW_TILE)
        value = reduced(ups_out, ups_in, at)
        dpre[rank, at, :] = (slope[at, :] * value).astype(bf16)

    each(tiles, dpre_tile)
    gather(DPRE, dpre)
    begin(GUP)

    def back_tile(index):
        at = span(index, ROW_TILE)
        block = gathered(dpre, at)
        for first in range(0, quarter, wide):
            columns = pl.ds(first, wide)
            back[at, columns] = dot(block, down[columns, :], (1, 1)).astype(bf16)

    each(tiles, back_tile)
    begin(BACK)

    def gdown_tile(owner):
        right = dpre[owner]
        for first in range(0, quarter, wide):
            columns = pl.ds(first, wide)
            gdown[owner, columns, :] = (dot(rows[:, columns], right, (0, 0)) * grad_scale).astype(
                bf16
            )

    each(OWN, gdown_tile)
    begin(GDOWN)
    for name in (GUP, OUT, GDOWN, BACK):
        finish(name)


def adapter(devices, grad_scale, tok, cot, down, w_up):
    bf16 = jnp.bfloat16
    slots, quarter = tok.shape
    units, width = w_up.shape
    hidden = units * OWN
    steps = max(devices // OWN, OWN)
    whole = pltpu.VMEM((OWN, slots, units), bf16)
    received = pltpu.VMEM((OWN - 1, slots, units), bf16)
    wide_rows = pltpu.VMEM((slots, quarter), bf16)
    return pl.pallas_call(
        functools.partial(adapter_kernel, devices, grad_scale),
        out_shape=[
            jax.ShapeDtypeStruct((slots, quarter), bf16),
            jax.ShapeDtypeStruct((slots, quarter), bf16),
            jax.ShapeDtypeStruct((width, units), bf16),
            jax.ShapeDtypeStruct((units, width), bf16),
        ],
        in_specs=[ANY] * 4,
        out_specs=[ANY] * 4,
        scratch_shapes=[
            wide_rows,
            wide_rows,
            pltpu.VMEM((quarter, hidden), bf16),
            pltpu.VMEM((hidden, quarter), bf16),
            whole,
            received,
            whole,
            received,
            whole,
            whole,
            pltpu.VMEM((slots, units), jnp.float32),
            wide_rows,
            wide_rows,
            pltpu.VMEM((OWN, units, quarter), bf16),
            pltpu.VMEM((OWN, quarter, units), bf16),
            pltpu.SemaphoreType.DMA((TRANSFERS, steps)),
            pltpu.SemaphoreType.DMA((TRANSFERS, steps)),
            pltpu.SemaphoreType.DMA((TRANSFERS,)),
        ],
        compiler_params=pltpu.CompilerParams(
            collective_id=2, has_side_effects=True, vmem_limit_bytes=48 * 1024 * 1024
        ),
    )(tok, cot, down, w_up)


def per_device(tokens, cotangent, block_lang, gain, w_down, w_up):
    bf16, f32 = jnp.bfloat16, jnp.float32
    devices = lax.axis_size("fsdp")
    languages = devices // OWN
    per_block, width = tokens.shape[1:]
    rows = per_block // languages
    quarter = width // OWN
    units = w_down.shape[1]
    hidden = units * OWN
    gain_width = gain.shape[0]
    slots = languages * MOSTB * rows
    grad_scale = 1.0 / math.sqrt(devices * per_block)
    me = lax.axis_index("fsdp")
    rank_here = lax.rem(me, OWN)

    ranks, table, filled = route_tables(block_lang, languages)
    home = tokens.reshape(per_block, width).astype(f32)
    home_cot = cotangent.reshape(per_block, width)
    root_mean = jnp.sqrt(jnp.mean(home * home, axis=-1, keepdims=True) + EPSILON)

    def slab(ref, peer):
        return ref.at[peer // OWN, :, span(lax.rem(peer, OWN), quarter)]

    def whole(ref, peer):
        return ref.at[0]

    def piece(ref, peer):
        return ref.at[peer // OWN]

    def at_device(ref, me):
        return ref.at[me]

    spread_tok, spread_cot, spread_root, gain_all, down = exchange(
        devices,
        1,
        [
            (
                "all",
                [
                    (2, piece, 2, at_device),
                    (3, whole, 3, at_device),
                    (0, slab, 0, at_device),
                    (1, slab, 1, at_device),
                ],
            ),
            (
                "owners",
                [
                    (
                        4,
                        lambda ref, peer: ref.at[span(lax.rem(peer, OWN), quarter), :],
                        4,
                        lambda ref, me: ref.at[:, span(lax.rem(me, OWN), units)],
                    )
                ],
            ),
        ],
        [
            tokens.reshape(languages, rows, width),
            cotangent.reshape(languages, rows, width),
            jnp.broadcast_to(root_mean, (per_block, 128)).reshape(languages, rows, 128),
            jnp.broadcast_to(gain, (1, 8, gain_width)),
            w_down,
        ],
        [
            ((devices, rows, quarter), bf16),
            ((devices, rows, quarter), bf16),
            ((devices, rows, 128), f32),
            ((devices, 8, gain_width), f32),
            ((quarter, units * OWN), bf16),
        ],
    )
    gain_full = gain_all[:, 0, :].reshape(width)
    gain_here = lax.dynamic_slice_in_dim(gain_full, rank_here * quarter, quarter)
    unit_rows = spread_tok.astype(f32) / spread_root[:, :, :1]
    normed = (unit_rows * gain_here).astype(bf16)

    def pick(values):
        return jnp.where(filled[:, :, None, None], values[table], jnp.zeros((), bf16))

    chunk = -(-MOSTB * rows // 16) * 16

    def packed(values):
        picked = pick(values).reshape(languages, MOSTB * rows, quarter)
        filler = ((0, 0), (0, chunk - MOSTB * rows), (0, 0))
        return jnp.pad(picked, filler).reshape(languages * chunk, quarter)

    def unpacked(values):
        shaped = values.reshape(languages, chunk, quarter)[:, : MOSTB * rows]
        return shaped.reshape(languages, MOSTB, rows, quarter)

    out_home, back_home, grad_down, grad_up = adapter(
        devices, grad_scale, packed(normed), packed(spread_cot), down, w_up
    )
    out_home, back_home = unpacked(out_home), unpacked(back_home)
    branch_rows = out_home[block_lang, ranks]
    dnormed_rows = back_home[block_lang, ranks]
    gain_part = jnp.sum(dnormed_rows.astype(f32) * unit_rows, axis=(0, 1))

    def at_home(ref, me):
        return ref.at[me // OWN, :, span(lax.rem(me, OWN), quarter)]

    branch, dnormed, gain_parts = exchange(
        devices,
        3,
        [
            (
                "all",
                [
                    (2, lambda ref, peer: ref.at[lax.rem(peer, languages)], 2, at_device),
                    (0, at_device, 0, at_home),
                    (1, at_device, 1, at_home),
                ],
            )
        ],
        [
            branch_rows,
            dnormed_rows,
            jnp.broadcast_to(
                gain_part.reshape(languages, 1, gain_width), (languages, 8, gain_width)
            ),
        ],
        [
            ((languages, rows, width), bf16),
            ((languages, rows, width), bf16),
            ((devices, 8, gain_width), f32),
        ],
    )
    holders = gain_parts[:, 0, :].reshape(languages, OWN, gain_width)
    grad_gain = (
        jnp.sum(
            lax.dynamic_index_in_dim(holders, me // languages, axis=1, keepdims=False), axis=0
        )
        * grad_scale
    )
    adapted = (home + branch.reshape(per_block, width).astype(f32)).astype(bf16)
    unit = home / root_mean
    scaled = dnormed.reshape(per_block, width).astype(f32) * gain_full
    inner = jnp.mean(scaled * unit, axis=-1, keepdims=True)
    x_grad = (home_cot.astype(f32) + (scaled - unit * inner) / root_mean).astype(bf16)
    return (
        adapted.reshape(tokens.shape),
        x_grad.reshape(tokens.shape),
        grad_down,
        grad_up,
        grad_gain,
    )


def solution(mesh):
    in_specs = (
        P(("groups", "fsdp"), None, None),
        P(("groups", "fsdp"), None, None),
        P("groups"),
        P("fsdp"),
        P(None, "fsdp"),
        P("fsdp", None),
    )
    out_specs = (
        P(("groups", "fsdp"), None, None),
        P(("groups", "fsdp"), None, None),
        P("groups", "fsdp"),
        P(("groups", "fsdp"), None),
        P(("groups", "fsdp")),
    )
    return jax.shard_map(
        per_device, mesh=mesh, in_specs=in_specs, out_specs=out_specs, check_vma=False
    )
```

```python
import functools
import math

import jax
import jax.numpy as jnp
from jax import lax
from jax.experimental import pallas as pl
from jax.experimental.pallas import tpu as pltpu
from jax.sharding import PartitionSpec as P

OWN = 4
MOSTB = 6
EPSILON = 1e-06
ANY = pl.BlockSpec(memory_space=pl.ANY)


def gelu_tanh(values):
    return jax.nn.gelu(values, approximate=True)


def route_tables(block_lang, languages):
    block_count = block_lang.shape[0]
    onehot = (block_lang[:, None] == jnp.arange(languages, dtype=jnp.int32)[None, :]).astype(
        jnp.int32
    )
    earlier = jnp.cumsum(onehot, axis=0) - onehot
    ranks = jnp.sum(earlier * onehot, axis=1)
    counts = jnp.sum(onehot, axis=0)
    places = jnp.arange(MOSTB, dtype=jnp.int32)
    matches = onehot[:, :, None] * (ranks[:, None, None] == places[None, None, :]).astype(jnp.int32)
    table = jnp.sum(matches * jnp.arange(block_count, dtype=jnp.int32)[:, None, None], axis=0)
    filled = places[None, :] < counts[:, None]
    return (ranks, table, filled)


def peer_of(kind, me, step, devices):
    if kind == "all":
        return lax.rem(me + step, devices)
    if kind == "across":
        return lax.rem(me + step * OWN, devices)
    return (me // OWN) * OWN + lax.rem(lax.rem(me, OWN) + step, OWN)


def size_of(kind, devices):
    return {"all": devices, "across": devices // OWN, "owners": OWN}[kind]


def exchange_kernel(devices, plans, n_in, n_out, *refs):
    ins, outs = refs[:n_in], refs[n_in : n_in + n_out]
    sems = refs[n_in + n_out :]
    me = lax.axis_index("fsdp")
    barrier = pltpu.get_barrier_semaphore()
    total = 0
    for kind, _ in plans:

        def greet(step, carry, kind=kind):
            pl.semaphore_signal(
                barrier,
                inc=1,
                device_id={"fsdp": peer_of(kind, me, step, devices)},
                device_id_type=pl.DeviceIdType.MESH,
            )
            return carry

        lax.fori_loop(1, size_of(kind, devices), greet, 0)
        total += size_of(kind, devices) - 1
    pl.semaphore_wait(barrier, total)

    def remote(at, index, step):
        kind, moves = plans[at]
        send, recv, _ = sems[3 * at : 3 * at + 3]
        source, take, target, put = moves[index]
        peer = peer_of(kind, me, step, devices)
        return pltpu.make_async_remote_copy(
            src_ref=take(ins[source], peer),
            dst_ref=put(outs[target], me),
            send_sem=send.at[index, step],
            recv_sem=recv.at[index, step],
            device_id={"fsdp": peer},
            device_id_type=pl.DeviceIdType.MESH,
        )

    def local(at, index):
        source, take, target, put = plans[at][1][index]
        own = sems[3 * at + 2]
        return pltpu.make_async_copy(take(ins[source], me), put(outs[target], me), own.at[index])

    for at, (kind, moves) in enumerate(plans):

        def begin(step, carry, at=at, moves=moves):
            for index in range(len(moves)):
                remote(at, index, step).start()
            return carry

        lax.fori_loop(1, size_of(kind, devices), begin, 0)
        for index in range(len(moves)):
            local(at, index).start()
    for at, (kind, moves) in enumerate(plans):

        def finish(step, carry, at=at, moves=moves):
            for index in range(len(moves)):
                remote(at, index, step).wait()
            return carry

        lax.fori_loop(1, size_of(kind, devices), finish, 0)
        for index in range(len(moves)):
            local(at, index).wait()


def exchange(devices, collective_id, plans, inputs, out_shapes):
    scratch = []
    for kind, moves in plans:
        count = size_of(kind, devices)
        scratch += [
            pltpu.SemaphoreType.DMA((len(moves), count)),
            pltpu.SemaphoreType.DMA((len(moves), count)),
            pltpu.SemaphoreType.DMA((len(moves),)),
        ]
    return pl.pallas_call(
        functools.partial(exchange_kernel, devices, plans, len(inputs), len(out_shapes)),
        out_shape=[jax.ShapeDtypeStruct(shape, dtype) for shape, dtype in out_shapes],
        in_specs=[ANY] * len(inputs),
        out_specs=[ANY] * len(out_shapes),
        scratch_shapes=scratch,
        compiler_params=pltpu.CompilerParams(
            collective_id=collective_id, has_side_effects=True
        ),
    )(*inputs)


def span(index, width):
    return pl.ds(pl.multiple_of(index * width, width), width)


ROW_TILE = 256
TRANSFERS = 12
TOK, COT, DOWN, UP, PRE, UPS, ACT, DPRE, OUT, BACK, GUP, GDOWN = range(TRANSFERS)
GELU_C = math.sqrt(2.0 / math.pi)


def adapter_kernel(
    devices, grad_scale, tok_ref, cot_ref, wd_ref, wu_ref, out_ref, back_ref, gd_ref, gu_ref,
    rows, cots, down, up, pre_out, pre_in, ups_out, ups_in, act, dpre, slope, out, back, gup, gdown,
    send, recv, own,
):
    bf16, f32 = jnp.bfloat16, jnp.float32
    me = lax.axis_index("fsdp")
    group, rank = me // OWN, lax.rem(me, OWN)
    languages = devices // OWN
    slots, quarter = rows.shape
    chunk = slots // languages
    units = wu_ref.shape[0]
    side, core = rank // 2, lax.rem(rank, 2)
    twin, facing, opposite = side * 2 + 1 - core, (1 - side) * 2 + core, (1 - side) * 2 + 1 - core
    wide = min(512, quarter)
    tiles = slots // ROW_TILE

    barrier = pltpu.get_barrier_semaphore()
    for kind in ("across", "owners"):

        def greet(step, carry, kind=kind):
            pl.semaphore_signal(
                barrier,
                inc=1,
                device_id={"fsdp": peer_of(kind, me, step, devices)},
                device_id_type=pl.DeviceIdType.MESH,
            )
            return carry

        lax.fori_loop(1, size_of(kind, devices), greet, 0)
    pl.semaphore_wait(barrier, languages - 1 + OWN - 1)

    def group_rows(ref):
        return lambda device, step: ref.at[span(device // OWN, chunk), :]

    def feature_columns(ref):
        return lambda device, step: ref.at[:, span(lax.rem(device, OWN), quarter)]

    def unit_rows(ref):
        return lambda device, step: ref.at[span(lax.rem(device, OWN), units), :]

    def by_rank(ref):
        return lambda device, step: ref.at[lax.rem(device, OWN)]

    moves = {
        TOK: ("across", group_rows(tok_ref), group_rows(rows), True),
        COT: ("across", group_rows(cot_ref), group_rows(cots), True),
        UP: ("owners", feature_columns(wu_ref), unit_rows(up), True),
        OUT: ("across", group_rows(out), group_rows(out_ref), True),
        BACK: ("across", group_rows(back), group_rows(back_ref), True),
        GUP: ("owners", by_rank(gup), feature_columns(gu_ref), True),
    }

    def remote(name, step):
        kind, take, put, _ = moves[name]
        peer = peer_of(kind, me, step, devices)
        return pltpu.make_async_remote_copy(
            src_ref=take(peer, step),
            dst_ref=put(me, step),
            send_sem=send.at[name, step],
            recv_sem=recv.at[name, step],
            device_id={"fsdp": peer},
            device_id_type=pl.DeviceIdType.MESH,
        )

    def local(name):
        _, take, put, _ = moves[name]
        return pltpu.make_async_copy(take(me, 0), put(me, 0), own.at[name])

    def begin(name):
        def body(step, carry):
            remote(name, step).start()
            return carry

        lax.fori_loop(1, size_of(moves[name][0], devices), body, 0)
        if moves[name][3]:
            local(name).start()

    def finish(name):
        def body(step, carry):
            remote(name, step).wait()
            return carry

        lax.fori_loop(1, size_of(moves[name][0], devices), body, 0)
        if moves[name][3]:
            local(name).wait()

    def direct(name, slot, source, target, rank_to):
        return pltpu.make_async_remote_copy(
            src_ref=source,
            dst_ref=target,
            send_sem=send.at[name, slot],
            recv_sem=recv.at[name, slot],
            device_id={"fsdp": group * OWN + rank_to},
            device_id_type=pl.DeviceIdType.MESH,
        )

    def reduce(name, parts, landed, beside=None):
        final = direct(name, 1, parts.at[twin], landed.at[0], twin)
        paired = direct(name, 2, parts.at[opposite], landed.at[1], twin)
        paired.start()
        final.start()
        paired.wait()

        def pair_tile(index):
            at = span(index, ROW_TILE)
            both = parts[facing, at, :].astype(f32) + landed[1, at, :].astype(f32)
            parts[facing, at, :] = both.astype(bf16)

        each(tiles, pair_tile)
        crossing = direct(name, 3, parts.at[facing], landed.at[2], facing)
        crossing.start()
        if beside is not None:
            beside()
        final.wait()
        crossing.wait()

    def reduced(parts, landed, at):
        value = parts[rank, at, :].astype(f32) + landed[0, at, :].astype(f32)
        return value + landed[2, at, :].astype(f32)

    def gather(name, ref, beside=None):
        across = direct(name, 2, ref.at[rank], ref.at[rank], facing)
        beside_me = direct(name, 1, ref.at[rank], ref.at[rank], twin)
        across.start()
        beside_me.start()
        if beside is not None:
            beside()
        across.wait()
        passed = direct(name, 3, ref.at[facing], ref.at[facing], twin)
        passed.start()
        beside_me.wait()
        passed.wait()

    def dot(left, right, over):
        return lax.dot_general(left, right, ((over[:1], over[1:]), ((), ())), preferred_element_type=f32)

    def each(count, body):
        def wrapped(index, carry):
            body(index)
            return carry

        lax.fori_loop(0, count, wrapped, 0)

    def gathered(ref, at):
        return jnp.concatenate([ref[owner, at, :] for owner in range(OWN)], axis=1)

    begin(TOK)
    begin(UP)
    load_down = pltpu.make_async_copy(wd_ref, down, own.at[DOWN])
    load_down.start()
    load_down.wait()
    finish(TOK)
    begin(COT)

    def pre_tile(index):
        at = span(index, ROW_TILE)
        block = rows[at, :]
        for owner in range(OWN):
            columns = pl.ds(owner * units, units)
            pre_out[owner, at, :] = dot(block, down[:, columns], (1, 0)).astype(bf16)

    each(tiles, pre_tile)
    reduce(PRE, pre_out, pre_in)

    def act_tile(index):
        at = span(index, ROW_TILE)
        value = reduced(pre_out, pre_in, at)
        square = value * value
        bent = jnp.tanh(GELU_C * (value + 0.044715 * (square * value)))
        half = 0.5 * (1.0 + bent)
        act[rank, at, :] = (value * half).astype(bf16)
        slope[at, :] = half + (0.5 * GELU_C) * value * (1.0 - bent * bent) * (
            1.0 + (3.0 * 0.044715) * square
        )

    each(tiles, act_tile)
    gather(ACT, act)
    finish(UP)

    def out_tile(index):
        at = span(index, ROW_TILE)
        block = gathered(act, at)
        for first in range(0, quarter, wide):
            columns = pl.ds(first, wide)
            out[at, columns] = dot(block, up[:, columns], (1, 0)).astype(bf16)

    each(tiles, out_tile)
    begin(OUT)
    finish(COT)

    def ups_tile(index):
        at = span(index, ROW_TILE)
        block = cots[at, :]
        for owner in range(OWN):
            ups_out[owner, at, :] = dot(block, up[pl.ds(owner * units, units), :], (1, 1)).astype(
                bf16
            )

    each(tiles, ups_tile)

    def gup_tile(owner):
        left = act[owner]
        for first in range(0, quarter, wide):
            columns = pl.ds(first, wide)
            gup[owner, :, columns] = (dot(left, cots[:, columns], (0, 0)) * grad_scale).astype(bf16)

    reduce(UPS, ups_out, ups_in, lambda: each(OWN, gup_tile))

    def dpre_tile(index):
        at = span(index, ROW_TILE)
        value = reduced(ups_out, ups_in, at)
        dpre[rank, at, :] = (slope[at, :] * value).astype(bf16)

    each(tiles, dpre_tile)
    gather(DPRE, dpre)
    begin(GUP)

    def back_tile(index):
        at = span(index, ROW_TILE)
        block = gathered(dpre, at)
        for first in range(0, quarter, wide):
            columns = pl.ds(first, wide)
            back[at, columns] = dot(block, down[columns, :], (1, 1)).astype(bf16)

    each(tiles, back_tile)
    begin(BACK)

    def gdown_tile(owner):
        right = dpre[owner]
        for first in range(0, quarter, wide):
            columns = pl.ds(first, wide)
            gdown[owner, columns, :] = (dot(rows[:, columns], right, (0, 0)) * grad_scale).astype(
                bf16
            )

    each(OWN, gdown_tile)
    store_gdown = pltpu.make_async_copy(gdown, gd_ref, own.at[GDOWN])
    store_gdown.start()
    for name in (GUP, OUT, BACK):
        finish(name)
    store_gdown.wait()


def adapter(devices, grad_scale, tok, cot, down, w_up):
    bf16 = jnp.bfloat16
    slots, quarter = tok.shape
    units, width = w_up.shape
    hidden = units * OWN
    steps = max(devices // OWN, OWN)
    whole = pltpu.VMEM((OWN, slots, units), bf16)
    received = pltpu.VMEM((OWN - 1, slots, units), bf16)
    wide_rows = pltpu.VMEM((slots, quarter), bf16)
    return pl.pallas_call(
        functools.partial(adapter_kernel, devices, grad_scale),
        out_shape=[
            jax.ShapeDtypeStruct((slots, quarter), bf16),
            jax.ShapeDtypeStruct((slots, quarter), bf16),
            jax.ShapeDtypeStruct((OWN, quarter, units), bf16),
            jax.ShapeDtypeStruct((units, width), bf16),
        ],
        in_specs=[ANY] * 4,
        out_specs=[ANY] * 4,
        scratch_shapes=[
            wide_rows,
            wide_rows,
            pltpu.VMEM((quarter, hidden), bf16),
            pltpu.VMEM((hidden, quarter), bf16),
            whole,
            received,
            whole,
            received,
            whole,
            whole,
            pltpu.VMEM((slots, units), jnp.float32),
            wide_rows,
            wide_rows,
            pltpu.VMEM((OWN, units, quarter), bf16),
            pltpu.VMEM((OWN, quarter, units), bf16),
            pltpu.SemaphoreType.DMA((TRANSFERS, steps)),
            pltpu.SemaphoreType.DMA((TRANSFERS, steps)),
            pltpu.SemaphoreType.DMA((TRANSFERS,)),
        ],
        compiler_params=pltpu.CompilerParams(
            collective_id=2, has_side_effects=True, vmem_limit_bytes=48 * 1024 * 1024
        ),
    )(tok, cot, down, w_up)


def per_device(tokens, cotangent, block_lang, gain, w_down, w_up):
    bf16, f32 = jnp.bfloat16, jnp.float32
    devices = lax.axis_size("fsdp")
    languages = devices // OWN
    per_block, width = tokens.shape[1:]
    rows = per_block // languages
    quarter = width // OWN
    units = w_down.shape[1]
    hidden = units * OWN
    gain_width = gain.shape[0]
    slots = languages * MOSTB * rows
    grad_scale = 1.0 / math.sqrt(devices * per_block)
    me = lax.axis_index("fsdp")
    rank_here = lax.rem(me, OWN)

    ranks, table, filled = route_tables(block_lang, languages)
    home = tokens.reshape(per_block, width).astype(f32)
    home_cot = cotangent.reshape(per_block, width)
    root_mean = jnp.sqrt(jnp.mean(home * home, axis=-1, keepdims=True) + EPSILON)

    def slab(ref, peer):
        return ref.at[peer // OWN, :, span(lax.rem(peer, OWN), quarter)]

    def whole(ref, peer):
        return ref.at[0]

    def piece(ref, peer):
        return ref.at[peer // OWN]

    def at_device(ref, me):
        return ref.at[me]

    spread_tok, spread_cot, spread_root, gain_all, down = exchange(
        devices,
        1,
        [
            (
                "all",
                [
                    (2, piece, 2, at_device),
                    (3, whole, 3, at_device),
                    (0, slab, 0, at_device),
                    (1, slab, 1, at_device),
                ],
            ),
            (
                "owners",
                [
                    (
                        4,
                        lambda ref, peer: ref.at[span(lax.rem(peer, OWN), quarter), :],
                        4,
                        lambda ref, me: ref.at[:, span(lax.rem(me, OWN), units)],
                    )
                ],
            ),
        ],
        [
            tokens.reshape(languages, rows, width),
            cotangent.reshape(languages, rows, width),
            jnp.broadcast_to(root_mean, (per_block, 128)).reshape(languages, rows, 128),
            jnp.broadcast_to(gain, (1, 8, gain_width)),
            w_down,
        ],
        [
            ((devices, rows, quarter), bf16),
            ((devices, rows, quarter), bf16),
            ((devices, rows, 128), f32),
            ((devices, 8, gain_width), f32),
            ((quarter, units * OWN), bf16),
        ],
    )
    gain_full = gain_all[:, 0, :].reshape(width)
    gain_here = lax.dynamic_slice_in_dim(gain_full, rank_here * quarter, quarter)
    unit_rows = spread_tok.astype(f32) / spread_root[:, :, :1]
    normed = (unit_rows * gain_here).astype(bf16)

    def pick(values):
        return jnp.where(filled[:, :, None, None], values[table], jnp.zeros((), bf16))

    chunk = -(-MOSTB * rows // 16) * 16

    def packed(values):
        picked = pick(values).reshape(languages, MOSTB * rows, quarter)
        filler = ((0, 0), (0, chunk - MOSTB * rows), (0, 0))
        return jnp.pad(picked, filler).reshape(languages * chunk, quarter)

    def unpacked(values):
        shaped = values.reshape(languages, chunk, quarter)[:, : MOSTB * rows]
        return shaped.reshape(languages, MOSTB, rows, quarter)

    out_home, back_home, part_grad_down, grad_up = adapter(
        devices, grad_scale, packed(normed), packed(spread_cot), down, w_up
    )
    out_home, back_home = unpacked(out_home), unpacked(back_home)
    branch_rows = out_home[block_lang, ranks]
    dnormed_rows = back_home[block_lang, ranks]
    gain_part = jnp.sum(dnormed_rows.astype(f32) * unit_rows, axis=(0, 1))

    def at_home(ref, me):
        return ref.at[me // OWN, :, span(lax.rem(me, OWN), quarter)]

    branch, dnormed, gain_parts, grad_down = exchange(
        devices,
        3,
        [
            (
                "all",
                [
                    (2, lambda ref, peer: ref.at[lax.rem(peer, languages)], 2, at_device),
                    (0, at_device, 0, at_home),
                    (1, at_device, 1, at_home),
                ],
            ),
            (
                "owners",
                [
                    (
                        3,
                        lambda ref, peer: ref.at[lax.rem(peer, OWN)],
                        3,
                        lambda ref, me: ref.at[span(lax.rem(me, OWN), quarter), :],
                    )
                ],
            ),
        ],
        [
            branch_rows,
            dnormed_rows,
            jnp.broadcast_to(
                gain_part.reshape(languages, 1, gain_width), (languages, 8, gain_width)
            ),
            part_grad_down,
        ],
        [
            ((languages, rows, width), bf16),
            ((languages, rows, width), bf16),
            ((devices, 8, gain_width), f32),
            ((width, units), bf16),
        ],
    )
    holders = gain_parts[:, 0, :].reshape(languages, OWN, gain_width)
    grad_gain = (
        jnp.sum(
            lax.dynamic_index_in_dim(holders, me // languages, axis=1, keepdims=False), axis=0
        )
        * grad_scale
    )
    adapted = (home + branch.reshape(per_block, width).astype(f32)).astype(bf16)
    unit = home / root_mean
    scaled = dnormed.reshape(per_block, width).astype(f32) * gain_full
    inner = jnp.mean(scaled * unit, axis=-1, keepdims=True)
    x_grad = (home_cot.astype(f32) + (scaled - unit * inner) / root_mean).astype(bf16)
    return (
        adapted.reshape(tokens.shape),
        x_grad.reshape(tokens.shape),
        grad_down,
        grad_up,
        grad_gain,
    )


def solution(mesh):
    in_specs = (
        P(("groups", "fsdp"), None, None),
        P(("groups", "fsdp"), None, None),
        P("groups"),
        P("fsdp"),
        P(None, "fsdp"),
        P("fsdp", None),
    )
    out_specs = (
        P(("groups", "fsdp"), None, None),
        P(("groups", "fsdp"), None, None),
        P("groups", "fsdp"),
        P(("groups", "fsdp"), None),
        P(("groups", "fsdp")),
    )
    return jax.shard_map(
        per_device, mesh=mesh, in_specs=in_specs, out_specs=out_specs, check_vma=False
    )
```
